32 devices in a mesh: grp: 2 (over x), sec: 8 (over z, y), head: 2 (over core).
Axes of the slice: x: 2, y: 2, z: 4, core: 2. Of those that a mesh axis runs over, the one named last changes fastest.
Arguments:
- patches: bfloat16 [4, 64, 1408], P('grp', 'head'), parts along dimension 0, may hold values from -6 to 6
- stale_kv: bfloat16 [16, 2, 512, 1408], P(('grp', 'sec'), None, None, 'head'), parts along dimension 0, as said below
- qkv_weight: bfloat16 [8, 3, 1408, 1408], P('sec', None, None, 'head'), may hold values from -0.15625 to 0.15625
- out_weight: bfloat16 [8, 1408, 1408], P('sec', 'head'), may hold values from -0.15625 to 0.15625
- skip_joined_weight: bfloat16 [8, 2816, 1408], P('sec'), may hold values from -0.109375 to 0.109375
- qk_gain: bfloat16 [8, 2, 1408], P('sec', None, 'head'), may hold values from 0.5 to 1.5
- order: int32 [16], P('grp'), parts along dimension 0, may hold values from 0 to 7, each once
- tile_index: int32 [2], P('grp'), parts along dimension 0, may hold values from 0 to 15
Outputs:
- section_out: bfloat16 [8, 4, 64, 1408], P('sec', 'grp', 'head'), parts along dimension 1
The draws below stay inside these ranges and needn't reach their ends.
There are 2 independent parts, one for each index of `grp`. The reference program is written for one: setup_inputs(seed, part) draws one part's arguments, and reference() takes and returns one part's arrays. A program takes and returns all parts, laid end to end along the dimension named above; an argument that names none is the same for every part. Nothing has to cross between parts.
Inputs may be any that keep to these rules, and one draw needn't show every extreme that they name: The first 2 entries name the slots of the patches, in the order of patches; all entries are distinct. `stale_kv`: in the key half, the 88 entries of each head of each row have a root mean square of at most 1.51.
All inputs are finite; a program needn't handle non-finite values.
Results may differ from the reference program's by a relative error of at most 0.018.
Values may be sent and summed in bfloat16 or wider, within the bound.
A program may use at most 64 MiB of HBM per device.

```python
import math
import jax
import jax.numpy as jnp
from jax import lax

D = 1408
HEADS = 16
HEAD_DIM = 88
PROWS = 64
PATCHES = 2
PATCH_SLOTS = 8
IMG_TILES = 16
TILE = 512
SECTIONS = 8


def draw_stale_kv(key, part):
    key_keys = jax.random.fold_in(key, 11)
    key_vals = jax.random.fold_in(key, 12)
    key_scale = jax.random.fold_in(key, 13)
    shape = (SECTIONS, TILE, HEADS, HEAD_DIM)
    raw = jax.random.normal(key_keys, shape, jnp.float32)
    scale_factors = jax.random.uniform(key_scale, (SECTIONS, TILE, HEADS, 1), jnp.float32, 0.5, 1.5)
    values = jax.random.normal(key_vals, (SECTIONS, TILE, D), jnp.float32)
    squares = jnp.mean(raw * raw, axis=-1, keepdims=True)
    keys_out = raw / jnp.sqrt(squares + 1e-06) * scale_factors
    stacked = jnp.stack([keys_out.reshape(SECTIONS, TILE, D), values], axis=1)
    return stacked.astype(jnp.bfloat16)


def level_of(stream_key, shape, shards, low, high):
    factor_of, own = 1.0, jax.random.fold_in(stream_key, 6)
    for dim, parts in shards:
        heights = jnp.exp(jax.random.uniform(jax.random.fold_in(own, dim), (parts,), jnp.float32, low / len(shards), high / len(shards)))
        factor_of = factor_of * jnp.repeat(heights, shape[dim] // parts).reshape([-1 if axis == dim else 1 for axis in range(len(shape))])
    return factor_of


def gaussian(own_key, dims, scale, most, split=(), kind=jnp.bfloat16):
    array = jax.random.normal(own_key, dims, jnp.float32) * scale
    if len(split) > 0:
        array = level_of(own_key, dims, split, -0.22, 0.18) * array
    return jnp.clip(array, min=-most, max=most).astype(kind)


def setup_inputs(seed: int = 0, part: int = 0) -> dict:
    splits = jax.random.split(jax.random.key(seed), 9)
    own_keys = jax.random.split(jax.random.fold_in(splits[8], part), 9)
    return {
        "patches": gaussian(own_keys[0], (PATCHES, PROWS, D), 1.0, 6.0, ((1, 2),)),
        "stale_kv": draw_stale_kv(jax.random.fold_in(jax.random.fold_in(splits[8], part), 71), part),
        "qkv_weight": gaussian(splits[2], (SECTIONS, 3, D, D), D ** -0.5, 0.15625, ((0, 8), (3, 2))),
        "out_weight": gaussian(splits[3], (SECTIONS, D, D), D ** -0.5, 0.15625, ((0, 8), (1, 2))),
        "skip_joined_weight": gaussian(splits[4], (SECTIONS, 2 * D, D), (2 * D) ** -0.5, 0.109375, ((0, 8),)),
        "qk_gain": jnp.clip(1.0 + 0.1 * jax.random.normal(splits[5], (SECTIONS, 2, D), jnp.float32), 0.5, 1.5).astype(jnp.bfloat16),
        "order": jax.random.permutation(own_keys[6], PATCH_SLOTS).astype(jnp.int32),
        "tile_index": jax.random.randint(own_keys[7], (1,), 0, IMG_TILES).astype(jnp.int32),
    }


EPSILON = 1e-06

def layer_norm(tensor):
    average = lax.optimization_barrier(jnp.mean(tensor, axis=-1, keepdims=True))
    centred = tensor - average
    variance = lax.optimization_barrier(jnp.mean(centred * centred, axis=-1, keepdims=True))
    return centred / jnp.sqrt(variance + EPSILON)

def rotate(tensor, position):
    half_width = tensor.shape[-1] // 2
    inverse = 10000.0 ** (-jnp.arange(half_width, dtype=jnp.float32) / half_width)
    angles = position[:, None] * inverse[None, :]
    cos_table = jnp.cos(angles)[:, None, :]
    sin_table = jnp.sin(angles)[:, None, :]
    leading = tensor[..., :half_width]
    trailing_half = tensor[..., half_width:]
    return jnp.concatenate([leading * cos_table - trailing_half * sin_table, leading * sin_table + trailing_half * cos_table], axis=-1)

def head_norm(projected, gain, position):
    row_count = projected.shape[0]
    heads_here = projected.shape[-1] // HEAD_DIM
    shaped = projected.reshape(row_count, heads_here, HEAD_DIM)
    scaled = layer_norm(shaped) * gain.astype(jnp.float32).reshape(heads_here, HEAD_DIM)
    return rotate(scaled, position).reshape(row_count, heads_here * HEAD_DIM).astype(jnp.bfloat16)

def attention_result(query_rot, key_cache, value_cache):
    row_count = query_rot.shape[0]
    heads_here = query_rot.shape[1] // HEAD_DIM
    query = query_rot.reshape(row_count, heads_here, HEAD_DIM).astype(jnp.float32)
    key_heads = key_cache.reshape(key_cache.shape[0], heads_here, HEAD_DIM).astype(jnp.float32)
    value_heads = value_cache.reshape(value_cache.shape[0], heads_here, HEAD_DIM).astype(jnp.float32)
    scores = jnp.einsum('qhd,khd->hqk', query, key_heads) / math.sqrt(HEAD_DIM)
    expd = jnp.exp(scores)
    weights = (expd / lax.optimization_barrier(jnp.sum(expd, axis=-1, keepdims=True))).astype(jnp.bfloat16)
    mixed = jnp.einsum('hqk,khd->qhd', weights.astype(jnp.float32), value_heads)
    return mixed.reshape(row_count, heads_here * HEAD_DIM).astype(jnp.bfloat16)

def reference(patches, stale_kv, qkv_weight, out_weight, skip_joined_weight, qk_gain, order, tile_index):
    sections = stale_kv.shape[0]
    half_count = sections // 2
    patch_count = patches.shape[0]
    patch_rows = patches.shape[1]
    tile_rows = stale_kv.shape[2]
    row_ids = jnp.arange(patch_rows, dtype=jnp.int32)
    finished = jnp.zeros((sections, patch_count, patch_rows, patches.shape[2]), jnp.bfloat16)
    for section in range(sections):
        key_cache = stale_kv[section, 0]
        value_cache = stale_kv[section, 1]
        produced_list = []
        for patch_idx in range(patch_count):
            source = patches[patch_idx] if section == 0 else finished[section - 1, patch_idx]
            if section >= half_count:
                skip_in = finished[sections - 1 - section, patch_idx]
                joined = jnp.concatenate([source, skip_in], axis=-1)
                mixed = jnp.dot(joined, skip_joined_weight[section], preferred_element_type=jnp.float32)
                residual = layer_norm(mixed).astype(jnp.bfloat16)
            else:
                residual = source
            normed = layer_norm(residual.astype(jnp.float32)).astype(jnp.bfloat16)
            query = jnp.dot(normed, qkv_weight[section, 0], preferred_element_type=jnp.float32)
            key_new = jnp.dot(normed, qkv_weight[section, 1], preferred_element_type=jnp.float32)
            value_raw = jnp.dot(normed, qkv_weight[section, 2], preferred_element_type=jnp.float32)
            row_start = (order[patch_idx] * patch_rows).astype(jnp.int32)
            position = (tile_index[0] * tile_rows + row_start + row_ids).astype(jnp.float32)
            query_rot = head_norm(query, qk_gain[section, 0], position)
            key_rot = head_norm(key_new, qk_gain[section, 1], position)
            value_new = value_raw.astype(jnp.bfloat16)
            key_cache = lax.dynamic_update_slice_in_dim(key_cache, key_rot, row_start, 0)
            value_cache = lax.dynamic_update_slice_in_dim(value_cache, value_new, row_start, 0)
            attended = attention_result(query_rot, key_cache, value_cache)
            update = jnp.dot(attended, out_weight[section], preferred_element_type=jnp.float32)
            produced_list.append((residual.astype(jnp.float32) + update).astype(jnp.bfloat16))
        finished = finished.at[section].set(jnp.stack(produced_list))
    return finished
```

```python
import functools
import math

import jax
import jax.numpy as jnp
import numpy as np
from jax import lax
from jax.experimental import pallas as pl
from jax.experimental.pallas import tpu as pltpu
from jax.sharding import PartitionSpec as P

HEAD_DIM = 88
EPSILON = 1e-06
LANES = 128
MESH = pl.DeviceIdType.MESH


def layer_norm(x):
    centred = x - jnp.mean(x, axis=-1, keepdims=True)
    variance = jnp.mean(centred * centred, axis=-1, keepdims=True)
    return centred * lax.rsqrt(variance + EPSILON)


def column_chunks(width, count):
    tiles = width // LANES
    step = -(-tiles // count)
    step += step % 2
    edges = list(range(0, tiles, step)) + [tiles]
    return [(a * LANES, (b - a) * LANES) for a, b in zip(edges[:-1], edges[1:])]


def kernel(
    dims,
    order_ref, tile_ref, patches_ref, gain_ref, freq_ref, kv_hbm, wqkv_hbm, wout_hbm, wskip_hbm,
    out_ref,
    wqkv, wout, wskip, kbuf, vbuf, ubuf, sbuf, pre, hsb, qs, ks, att, pbuf, psend, precv, obuf, cosb, sinb, gains,
    w_sem, kv_sem, wo_sem, ws_sem,
    u_send, u_recv, r_send, r_recv, s_send, s_recv, t_send, t_recv, p_send, p_recv,
):
    sections, patch_count, own_rows, width, lanes, tile_rows, chunks = dims
    rows = own_rows * 2
    heads = lanes // HEAD_DIM
    wide = qs.shape[1]
    half = sections // 2
    last = sections - 1
    sec = lax.axis_index("sec")
    core = lax.axis_index("head")
    peer = 1 - core
    partner = last - sec
    own = pl.ds(pl.multiple_of(core * own_rows, own_rows), own_rows)
    other = pl.ds(pl.multiple_of(peer * own_rows, own_rows), own_rows)
    far_partner = (sec < half - 1) | (sec > half)

    w_copies = [pltpu.make_async_copy(wqkv_hbm.at[0, c], wqkv.at[c], w_sem.at[c]) for c in range(3)]
    k_copy = pltpu.make_async_copy(kv_hbm.at[0, 0], kbuf.at[pl.ds(0, tile_rows)], kv_sem.at[0])
    v_copy = pltpu.make_async_copy(kv_hbm.at[0, 1], vbuf.at[pl.ds(0, tile_rows)], kv_sem.at[1])
    o_copy = pltpu.make_async_copy(wout_hbm.at[0], wout, wo_sem)
    top_copy = pltpu.make_async_copy(wskip_hbm.at[0, pl.ds(0, width)], wskip.at[pl.ds(0, width)], ws_sem.at[0])
    low_copy = pltpu.make_async_copy(wskip_hbm.at[0, pl.ds(width, width)], wskip.at[pl.ds(width, width)], ws_sem.at[1])
    for copy in (*w_copies, k_copy, v_copy, o_copy):
        copy.start()

    @pl.when(sec >= half)
    def _():
        low_copy.start()
        top_copy.start()

    barrier = pltpu.get_barrier_semaphore()
    pl.semaphore_signal(barrier, inc=1, device_id={"head": peer}, device_id_type=MESH)

    @pl.when(sec < last)
    def _():
        pl.semaphore_signal(barrier, inc=1, device_id={"sec": sec + 1}, device_id_type=MESH)

    @pl.when(sec > 0)
    def _():
        pl.semaphore_signal(barrier, inc=1, device_id={"sec": sec - 1}, device_id_type=MESH)

    @pl.when(far_partner)
    def _():
        pl.semaphore_signal(barrier, inc=1, device_id={"sec": partner}, device_id_type=MESH)

    greeted = (
        1
        + jnp.where(sec < last, 1, 0)
        + jnp.where(sec > 0, 1, 0)
        + jnp.where(far_partner, 1, 0)
    )
    pl.semaphore_wait(barrier, greeted)

    def relay_u(k, j):
        start, size = chunks[j]
        piece = ubuf.at[k, own, pl.ds(start, size)]
        return pltpu.make_async_remote_copy(
            piece, piece, r_send.at[k, j], r_recv.at[k, j], device_id={"head": peer}, device_id_type=MESH
        )

    def send_u(k, j):
        start, size = chunks[j]
        return pltpu.make_async_remote_copy(
            obuf.at[k, :, pl.ds(start, size)],
            ubuf.at[k, own, pl.ds(start, size)],
            u_send.at[k, j],
            u_recv.at[k, j],
            device_id={"sec": jnp.minimum(sec + 1, last)},
            device_id_type=MESH,
        )

    def send_skip(k):
        return pltpu.make_async_remote_copy(
            obuf.at[k], sbuf.at[k, own], s_send.at[k], s_recv.at[k], device_id={"sec": partner}, device_id_type=MESH
        )

    def relay_skip(k):
        piece = sbuf.at[k, own]
        return pltpu.make_async_remote_copy(
            piece, piece, t_send.at[k], t_recv.at[k], device_id={"head": peer}, device_id_type=MESH
        )

    def send_part(k, j):
        start, size = chunks[j]
        return pltpu.make_async_remote_copy(
            psend.at[k, :, pl.ds(start, size)],
            precv.at[k, :, pl.ds(start, size)],
            p_send.at[k, j],
            p_recv.at[k, j],
            device_id={"head": peer},
            device_id_type=MESH,
        )

    @pl.when(sec == 0)
    def _():
        for k in range(patch_count):
            ubuf[k, own, :] = patches_ref[k]

    tiles = [(t, min(LANES, lanes - t)) for t in range(0, lanes, LANES)]
    lane = [lax.broadcasted_iota(jnp.int32, (1, LANES), 1) + t for t, _ in tiles]

    def spans(h):
        return [t for t in range(len(tiles)) if t * LANES < (h + 1) * HEAD_DIM and (t + 1) * LANES > h * HEAD_DIM]

    def mask(h, t):
        return (lane[t] >= h * HEAD_DIM) & (lane[t] < (h + 1) * HEAD_DIM)

    def tables(k, _):
        start = tile_ref[0] * tile_rows + order_ref[k] * rows
        position = (lax.broadcasted_iota(jnp.int32, (rows, LANES), 0) + start).astype(jnp.float32)
        for t in range(len(tiles)):
            cols = pl.ds(t * LANES, LANES)
            angle = position * freq_ref[0:1, cols]
            cosb[k, :, cols] = jnp.cos(angle)
            sinb[k, :, cols] = jnp.sin(angle) * freq_ref[1:2, cols]
        return 0

    lax.fori_loop(0, patch_count, tables, 0)
    qs[...] = jnp.zeros_like(qs)
    ks[...] = jnp.zeros_like(ks)
    gains[...] = jnp.zeros_like(gains)
    gains[:, pl.ds(0, lanes)] = gain_ref[0].astype(jnp.float32)
    kbuf[pl.ds(tile_rows, rows * patch_count), :] = jnp.zeros((rows * patch_count, lanes), jnp.bfloat16)
    vbuf[pl.ds(tile_rows, rows * patch_count), :] = jnp.zeros((rows * patch_count, lanes), jnp.bfloat16)

    @pl.when(sec >= half)
    def _():
        low_copy.wait()

    @pl.when(sec > half)
    def _():
        def ahead(k, _):
            relay = relay_skip(k)
            send_skip(k).wait_recv()
            relay.start()
            relay.wait_recv()
            pre[k] = jnp.dot(sbuf[k], wskip[pl.ds(width, width), :], preferred_element_type=jnp.float32)
            return 0

        lax.fori_loop(0, patch_count, ahead, 0)

    @pl.when(sec >= half)
    def _():
        top_copy.wait()

    def head_sums(parts):
        sums = [None] * heads
        for h in range(heads):
            total = None
            for t in spans(h):
                term = jnp.where(mask(h, t), parts[t], 0.0)
                total = term if total is None else total + term
            sums[h] = jnp.sum(total, axis=1, keepdims=True) * (1.0 / HEAD_DIM)
        result = []
        for t in range(len(tiles)):
            value = jnp.zeros((rows, LANES), jnp.float32)
            for h in range(heads):
                if t in spans(h):
                    value = jnp.where(mask(h, t), sums[h], value)
            result.append(value)
        return result

    def head_norm(buf, which, k):
        parts = [buf[:, pl.ds(t * LANES, LANES)] for t in range(len(tiles))]
        means = head_sums(parts)
        parts = [a - m for a, m in zip(parts, means)]
        variances = head_sums([a * a for a in parts])
        for t in range(len(tiles)):
            cols = pl.ds(t * LANES, LANES)
            buf[:, cols] = parts[t] * lax.rsqrt(variances[t] + EPSILON) * gains[which : which + 1, cols]
        value = buf[...]
        ahead = pltpu.roll(value, wide - HEAD_DIM // 2, 1)
        behind = pltpu.roll(value, HEAD_DIM // 2, 1)
        turned = jnp.where(freq_ref[1:2, :] < 0.0, ahead, behind)
        return value * cosb[k] + turned * sinb[k]

    def step(k, _):
        for j in range(len(chunks)):
            @pl.when(sec > 0)
            def _():
                send_u(k, j).wait_recv()

            relay_u(k, j).start()
        for j in range(len(chunks)):
            relay_u(k, j).wait_recv()

        @pl.when(sec < half)
        def _():
            hsb[...] = ubuf[k]

        @pl.when(sec == half)
        def _():
            pre[k] = jnp.dot(ubuf[k], wskip[pl.ds(width, width), :], preferred_element_type=jnp.float32)

        @pl.when(sec >= half)
        def _():
            mixed = pre[k] + jnp.dot(ubuf[k], wskip[pl.ds(0, width), :], preferred_element_type=jnp.float32)
            hsb[...] = layer_norm(mixed).astype(jnp.bfloat16)

        normed = layer_norm(hsb[...].astype(jnp.float32)).astype(jnp.bfloat16)

        @pl.when(k == 0)
        def _():
            for copy in (*w_copies, k_copy, v_copy, o_copy):
                copy.wait()

        qs[:, pl.ds(0, lanes)] = jnp.dot(normed, wqkv[0], preferred_element_type=jnp.float32)
        ks[:, pl.ds(0, lanes)] = jnp.dot(normed, wqkv[1], preferred_element_type=jnp.float32)
        fresh = pl.ds(pl.multiple_of(tile_rows + k * rows, rows), rows)
        vbuf[fresh, :] = jnp.dot(normed, wqkv[2], preferred_element_type=jnp.float32).astype(jnp.bfloat16)
        q_rot = head_norm(qs, 0, k)
        k_rot = head_norm(ks, 1, k)
        kbuf[fresh, :] = k_rot[:, :lanes].astype(jnp.bfloat16)

        keys = tile_rows + patch_count * rows
        column = lax.broadcasted_iota(jnp.int32, (1, keys), 1)
        slot = column // rows
        stale_slots = tile_rows // rows
        gone = slot > stale_slots + k
        for i in range(patch_count):
            gone = gone | ((slot == order_ref[i]) & (i <= k))
        keep = jnp.where(gone, 0.0, 1.0)
        scale = math.log2(math.e) / math.sqrt(HEAD_DIM)
        mixed_tiles = [None] * len(tiles)
        for h in range(heads):
            found = spans(h)
            low = found[0] * LANES
            span = min(lanes, (found[-1] + 1) * LANES) - low
            query = jnp.concatenate(
                [jnp.where(mask(h, t), q_rot[:, t * LANES : (t + 1) * LANES], 0.0) for t in found], axis=1
            )[:, :span].astype(jnp.bfloat16)
            window = pl.ds(low, span)
            scores = lax.dot_general(
                query, kbuf[:, window], (((1,), (1,)), ((), ())), preferred_element_type=jnp.float32
            )
            expd = jnp.exp2(scores * scale) * keep
            inverse = 1.0 / jnp.sum(expd, axis=1, keepdims=True)
            mixed = jnp.dot(expd.astype(jnp.bfloat16), vbuf[:, window], preferred_element_type=jnp.float32) * inverse
            for t in found:
                size = tiles[t][1]
                value = mixed[:, t * LANES - low : t * LANES - low + size]
                before = mixed_tiles[t]
                mixed_tiles[t] = value if before is None else jnp.where(mask(h, t)[:, :size], value, before)
        for t, (begin, size) in enumerate(tiles):
            att[:, pl.ds(begin, size)] = mixed_tiles[t].astype(jnp.bfloat16)

        for j, (begin, size) in enumerate(chunks):
            cols = pl.ds(begin, size)
            pbuf[:, cols] = jnp.dot(att[...], wout[:, cols], preferred_element_type=jnp.float32)
            psend[k, :, cols] = pbuf[other, cols].astype(jnp.bfloat16)
            send_part(k, j).start()
        for j, (begin, size) in enumerate(chunks):
            cols = pl.ds(begin, size)
            mine = hsb[own, cols].astype(jnp.float32) + pbuf[own, cols]
            send_part(k, j).wait_recv()
            produced = (mine + precv[k, :, cols].astype(jnp.float32)).astype(jnp.bfloat16)
            obuf[k, :, cols] = produced

            @pl.when(sec < last)
            def _():
                send_u(k, j).start()

            out_ref[0, k, :, cols] = produced

        @pl.when(sec < half - 1)
        def _():
            send_skip(k).start()

        return 0

    lax.fori_loop(0, patch_count, step, 0)

    def finish(k, _):
        for j in range(len(chunks)):
            relay_u(k, j).wait_send()
            send_part(k, j).wait_send()

            @pl.when(sec < last)
            def _():
                send_u(k, j).wait_send()

        @pl.when(sec < half - 1)
        def _():
            send_skip(k).wait_send()

        @pl.when(sec > half)
        def _():
            relay_skip(k).wait_send()

        return 0

    lax.fori_loop(0, patch_count, finish, 0)


def body(patches, stale_kv, qkv_weight, out_weight, skip_joined_weight, qk_gain, order, tile_index):
    patch_count, own_rows, width = patches.shape
    sections = lax.axis_size("sec")
    tile_rows, lanes = stale_kv.shape[2:]
    rows = own_rows * 2
    wide = -(-lanes // LANES) * LANES
    chunks = column_chunks(width, 2)
    keys = tile_rows + patch_count * rows
    half_width = HEAD_DIM // 2
    index = np.arange(wide) % HEAD_DIM
    inverse = 10000.0 ** (-(index % half_width).astype(np.float64) / half_width)
    sign = np.where(index < half_width, -1.0, 1.0)
    freq = jnp.asarray(np.stack([inverse, sign]).astype(np.float32))
    count = len(chunks)
    bf, f32 = jnp.bfloat16, jnp.float32
    vmem = pl.BlockSpec(memory_space=pltpu.VMEM)
    smem = pl.BlockSpec(memory_space=pltpu.SMEM)
    hbm = pl.BlockSpec(memory_space=pl.ANY)
    dma = pltpu.SemaphoreType.DMA
    dims = (sections, patch_count, own_rows, width, lanes, tile_rows, chunks)
    return pl.pallas_call(
        functools.partial(kernel, dims),
        out_shape=jax.ShapeDtypeStruct((1, patch_count, own_rows, width), bf),
        in_specs=[smem, smem, vmem, vmem, vmem, hbm, hbm, hbm, hbm],
        out_specs=vmem,
        scratch_shapes=[
            pltpu.VMEM((3, width, lanes), bf),
            pltpu.VMEM((lanes, width), bf),
            pltpu.VMEM((2 * width, width), bf),
            pltpu.VMEM((keys, lanes), bf),
            pltpu.VMEM((keys, lanes), bf),
            pltpu.VMEM((patch_count, rows, width), bf),
            pltpu.VMEM((patch_count, rows, width), bf),
            pltpu.VMEM((patch_count, rows, width), f32),
            pltpu.VMEM((rows, width), bf),
            pltpu.VMEM((rows, wide), f32),
            pltpu.VMEM((rows, wide), f32),
            pltpu.VMEM((rows, lanes), bf),
            pltpu.VMEM((rows, width), f32),
            pltpu.VMEM((patch_count, own_rows, width), bf),
            pltpu.VMEM((patch_count, own_rows, width), bf),
            pltpu.VMEM((patch_count, own_rows, width), bf),
            pltpu.VMEM((patch_count, rows, wide), f32),
            pltpu.VMEM((patch_count, rows, wide), f32),
            pltpu.VMEM((2, wide), f32),
            dma((3,)),
            dma((2,)),
            dma,
            dma((2,)),
            dma((patch_count, count)),
            dma((patch_count, count)),
            dma((patch_count, count)),
            dma((patch_count, count)),
            dma((patch_count,)),
            dma((patch_count,)),
            dma((patch_count,)),
            dma((patch_count,)),
            dma((patch_count, count)),
            dma((patch_count, count)),
        ],
        compiler_params=pltpu.CompilerParams(
            collective_id=0, has_side_effects=True, vmem_limit_bytes=44 * 1024 * 1024
        ),
    )(order, tile_index, patches, qk_gain, freq, stale_kv, qkv_weight, out_weight, skip_joined_weight)


def solution(mesh):
    return jax.shard_map(
        body,
        mesh=mesh,
        in_specs=(
            P("grp", "head", None),
            P(("grp", "sec"), None, None, "head"),
            P("sec", None, None, "head"),
            P("sec", "head", None),
            P("sec", None, None),
            P("sec", None, "head"),
            P("grp"),
            P("grp"),
        ),
        out_specs=P("sec", "grp", "head", None),
        check_vma=False,
    )
```

```python
import functools
import math

import jax
import jax.numpy as jnp
import numpy as np
from jax import lax
from jax.experimental import pallas as pl
from jax.experimental.pallas import tpu as pltpu
from jax.sharding import PartitionSpec as P

HEAD_DIM = 88
EPSILON = 1e-06
LANES = 128
MESH = pl.DeviceIdType.MESH


def layer_norm(x):
    centred = x - jnp.mean(x, axis=-1, keepdims=True)
    variance = jnp.mean(centred * centred, axis=-1, keepdims=True)
    return centred * lax.rsqrt(variance + EPSILON)


def across(a, b):
    return lax.dot_general(a, b, (((1,), (1,)), ((), ())), preferred_element_type=jnp.float32)


def column_chunks(width, count):
    tiles = width // LANES
    step = -(-tiles // count)
    step += step % 2
    edges = list(range(0, tiles, step)) + [tiles]
    return [(a * LANES, (b - a) * LANES) for a, b in zip(edges[:-1], edges[1:])]


def kernel(
    dims,
    order_ref, tile_ref, patches_hbm, gain_hbm, freq_hbm, kv_hbm, wqkv_hbm, wout_hbm, wskip_hbm,
    out_ref,
    patches_ref, gain_ref, freq_ref, wqkv, wout, wskip, kbuf, vbuf, knew, vnew, ubuf, sbuf, pre, hsb, qs, ks, att, pbuf, psend, precv, obuf, cosb, sinb, gains,
    in_sem, w_sem, kv_sem, wo_sem, ws_sem,
    u_send, u_recv, r_send, r_recv, s_send, s_recv, t_send, t_recv, p_send, p_recv,
):
    sections, patch_count, own_rows, width, lanes, tile_rows, chunks = dims
    rows = own_rows * 2
    heads = lanes // HEAD_DIM
    wide = qs.shape[1]
    half = sections // 2
    last = sections - 1
    sec = lax.axis_index("sec")
    core = lax.axis_index("head")
    peer = 1 - core
    partner = last - sec
    own = pl.ds(pl.multiple_of(core * own_rows, own_rows), own_rows)
    other = pl.ds(pl.multiple_of(peer * own_rows, own_rows), own_rows)
    far_partner = (sec < half - 1) | (sec > half)

    w_copies = [pltpu.make_async_copy(wqkv_hbm.at[0, c], wqkv.at[c], w_sem.at[c]) for c in range(3)]
    k_copy = pltpu.make_async_copy(kv_hbm.at[0, 0], kbuf, kv_sem.at[0])
    v_copy = pltpu.make_async_copy(kv_hbm.at[0, 1], vbuf, kv_sem.at[1])
    o_copy = pltpu.make_async_copy(wout_hbm.at[0], wout, wo_sem)
    top_copy = pltpu.make_async_copy(wskip_hbm.at[0, pl.ds(0, width)], wskip.at[pl.ds(0, width)], ws_sem.at[0])
    low_copy = pltpu.make_async_copy(wskip_hbm.at[0, pl.ds(width, width)], wskip.at[pl.ds(width, width)], ws_sem.at[1])
    small = [
        pltpu.make_async_copy(patches_hbm, patches_ref, in_sem.at[0]),
        pltpu.make_async_copy(freq_hbm, freq_ref, in_sem.at[1]),
        pltpu.make_async_copy(gain_hbm, gain_ref, in_sem.at[2]),
    ]
    for copy in (*small, *w_copies, k_copy, v_copy, o_copy):
        copy.start()

    @pl.when(sec >= half)
    def _():
        low_copy.start()
        top_copy.start()

    barrier = pltpu.get_barrier_semaphore()
    pl.semaphore_signal(barrier, inc=1, device_id={"head": peer}, device_id_type=MESH)

    @pl.when(sec < last)
    def _():
        pl.semaphore_signal(barrier, inc=1, device_id={"sec": sec + 1}, device_id_type=MESH)

    @pl.when(sec > 0)
    def _():
        pl.semaphore_signal(barrier, inc=1, device_id={"sec": sec - 1}, device_id_type=MESH)

    @pl.when(far_partner)
    def _():
        pl.semaphore_signal(barrier, inc=1, device_id={"sec": partner}, device_id_type=MESH)

    greeted = (
        1
        + jnp.where(sec < last, 1, 0)
        + jnp.where(sec > 0, 1, 0)
        + jnp.where(far_partner, 1, 0)
    )
    pl.semaphore_wait(barrier, greeted)

    def relay_u(k, j):
        start, size = chunks[j]
        piece = ubuf.at[k, own, pl.ds(start, size)]
        return pltpu.make_async_remote_copy(
            piece, piece, r_send.at[k, j], r_recv.at[k, j], device_id={"head": peer}, device_id_type=MESH
        )

    def send_u(k, j):
        start, size = chunks[j]
        return pltpu.make_async_remote_copy(
            obuf.at[k, :, pl.ds(start, size)],
            ubuf.at[k, own, pl.ds(start, size)],
            u_send.at[k, j],
            u_recv.at[k, j],
            device_id={"sec": jnp.minimum(sec + 1, last)},
            device_id_type=MESH,
        )

    def send_skip(k):
        return pltpu.make_async_remote_copy(
            obuf.at[k], sbuf.at[k, own], s_send.at[k], s_recv.at[k], device_id={"sec": partner}, device_id_type=MESH
        )

    def relay_skip(k):
        piece = sbuf.at[k, own]
        return pltpu.make_async_remote_copy(
            piece, piece, t_send.at[k], t_recv.at[k], device_id={"head": peer}, device_id_type=MESH
        )

    def send_part(k, j):
        start, size = chunks[j]
        return pltpu.make_async_remote_copy(
            psend.at[k, :, pl.ds(start, size)],
            precv.at[k, :, pl.ds(start, size)],
            p_send.at[k, j],
            p_recv.at[k, j],
            device_id={"head": peer},
            device_id_type=MESH,
        )

    for copy in small:
        copy.wait()

    @pl.when(sec == 0)
    def _():
        for k in range(patch_count):
            ubuf[k, own, :] = patches_ref[k]

    tiles = [(t, min(LANES, lanes - t)) for t in range(0, lanes, LANES)]
    lane = [lax.broadcasted_iota(jnp.int32, (1, LANES), 1) + t for t, _ in tiles]

    def spans(h):
        return [t for t in range(len(tiles)) if t * LANES < (h + 1) * HEAD_DIM and (t + 1) * LANES > h * HEAD_DIM]

    def mask(h, t):
        return (lane[t] >= h * HEAD_DIM) & (lane[t] < (h + 1) * HEAD_DIM)

    def tables(k, _):
        start = tile_ref[0] * tile_rows + order_ref[k] * rows
        position = (lax.broadcasted_iota(jnp.int32, (rows, LANES), 0) + start).astype(jnp.float32)
        for t in range(len(tiles)):
            cols = pl.ds(t * LANES, LANES)
            angle = position * freq_ref[0:1, cols]
            cosb[k, :, cols] = jnp.cos(angle)
            sinb[k, :, cols] = jnp.sin(angle) * freq_ref[1:2, cols]
        return 0

    lax.fori_loop(0, patch_count, tables, 0)
    qs[...] = jnp.zeros_like(qs)
    ks[...] = jnp.zeros_like(ks)
    gains[...] = jnp.zeros_like(gains)
    gains[:, pl.ds(0, lanes)] = gain_ref[0].astype(jnp.float32)
    knew[...] = jnp.zeros_like(knew)
    vnew[...] = jnp.zeros_like(vnew)

    @pl.when(sec >= half)
    def _():
        low_copy.wait()

    @pl.when(sec > half)
    def _():
        def ahead(k, _):
            relay = relay_skip(k)
            send_skip(k).wait_recv()
            relay.start()
            relay.wait_recv()
            pre[k] = jnp.dot(sbuf[k], wskip[pl.ds(width, width), :], preferred_element_type=jnp.float32)
            return 0

        lax.fori_loop(0, patch_count, ahead, 0)

    @pl.when(sec >= half)
    def _():
        top_copy.wait()

    def head_sums(parts):
        sums = [None] * heads
        for h in range(heads):
            total = None
            for t in spans(h):
                term = jnp.where(mask(h, t), parts[t], 0.0)
                total = term if total is None else total + term
            sums[h] = jnp.sum(total, axis=1, keepdims=True) * (1.0 / HEAD_DIM)
        result = []
        for t in range(len(tiles)):
            value = jnp.zeros((rows, LANES), jnp.float32)
            for h in range(heads):
                if t in spans(h):
                    value = jnp.where(mask(h, t), sums[h], value)
            result.append(value)
        return result

    def head_norm(buf, which, k):
        parts = [buf[:, pl.ds(t * LANES, LANES)] for t in range(len(tiles))]
        means = head_sums(parts)
        parts = [a - m for a, m in zip(parts, means)]
        variances = head_sums([a * a for a in parts])
        for t in range(len(tiles)):
            cols = pl.ds(t * LANES, LANES)
            buf[:, cols] = parts[t] * lax.rsqrt(variances[t] + EPSILON) * gains[which : which + 1, cols]
        value = buf[...]
        ahead = pltpu.roll(value, wide - HEAD_DIM // 2, 1)
        behind = pltpu.roll(value, HEAD_DIM // 2, 1)
        turned = jnp.where(freq_ref[1:2, :] < 0.0, ahead, behind)
        return value * cosb[k] + turned * sinb[k]

    def step(k, _):
        for j in range(len(chunks)):
            @pl.when(sec > 0)
            def _():
                send_u(k, j).wait_recv()

            relay_u(k, j).start()
        for j in range(len(chunks)):
            relay_u(k, j).wait_recv()

        @pl.when(sec < half)
        def _():
            hsb[...] = ubuf[k]

        @pl.when(sec == half)
        def _():
            pre[k] = jnp.dot(ubuf[k], wskip[pl.ds(width, width), :], preferred_element_type=jnp.float32)

        @pl.when(sec >= half)
        def _():
            mixed = pre[k] + jnp.dot(ubuf[k], wskip[pl.ds(0, width), :], preferred_element_type=jnp.float32)
            hsb[...] = layer_norm(mixed).astype(jnp.bfloat16)

        normed = layer_norm(hsb[...].astype(jnp.float32)).astype(jnp.bfloat16)

        @pl.when(k == 0)
        def _():
            for copy in (*w_copies, k_copy, v_copy, o_copy):
                copy.wait()

        qs[:, pl.ds(0, lanes)] = across(normed, wqkv[0])
        ks[:, pl.ds(0, lanes)] = across(normed, wqkv[1])
        fresh = pl.ds(pl.multiple_of(k * rows, rows), rows)
        vnew[fresh, :] = across(normed, wqkv[2]).astype(jnp.bfloat16)
        q_rot = head_norm(qs, 0, k)
        k_rot = head_norm(ks, 1, k)
        knew[fresh, :] = k_rot[:, :lanes].astype(jnp.bfloat16)

        slot = lax.broadcasted_iota(jnp.int32, (1, tile_rows), 1) // rows
        gone = slot < 0
        for i in range(patch_count):
            gone = gone | ((slot == order_ref[i]) & (i <= k))
        keep = jnp.where(gone, 0.0, 1.0)
        source = lax.broadcasted_iota(jnp.int32, (1, patch_count * rows), 1) // rows
        keep_new = jnp.where(source > k, 0.0, 1.0)
        scale = math.log2(math.e) / math.sqrt(HEAD_DIM)
        mixed_tiles = [None] * len(tiles)
        for h in range(heads):
            found = spans(h)
            low = found[0] * LANES
            span = min(lanes, (found[-1] + 1) * LANES) - low
            query = jnp.concatenate(
                [jnp.where(mask(h, t), q_rot[:, t * LANES : (t + 1) * LANES], 0.0) for t in found], axis=1
            )[:, :span].astype(jnp.bfloat16)
            window = pl.ds(low, span)
            scores = jnp.dot(query, kbuf[window, :], preferred_element_type=jnp.float32)
            scores_new = across(query, knew[:, window])
            expd = jnp.exp2(scores * scale) * keep
            expd_new = jnp.exp2(scores_new * scale) * keep_new
            total = jnp.sum(expd, axis=1, keepdims=True) + jnp.sum(expd_new, axis=1, keepdims=True)
            mixed = across(expd.astype(jnp.bfloat16), vbuf[window, :]) + jnp.dot(
                expd_new.astype(jnp.bfloat16), vnew[:, window], preferred_element_type=jnp.float32
            )
            mixed = mixed * (1.0 / total)
            for t in found:
                size = tiles[t][1]
                value = mixed[:, t * LANES - low : t * LANES - low + size]
                before = mixed_tiles[t]
                mixed_tiles[t] = value if before is None else jnp.where(mask(h, t)[:, :size], value, before)
        for t, (begin, size) in enumerate(tiles):
            att[:, pl.ds(begin, size)] = mixed_tiles[t].astype(jnp.bfloat16)

        for j, (begin, size) in enumerate(chunks):
            cols = pl.ds(begin, size)
            pbuf[:, cols] = jnp.dot(att[...], wout[:, cols], preferred_element_type=jnp.float32)
            psend[k, :, cols] = pbuf[other, cols].astype(jnp.bfloat16)
            send_part(k, j).start()
        for j, (begin, size) in enumerate(chunks):
            cols = pl.ds(begin, size)
            mine = hsb[own, cols].astype(jnp.float32) + pbuf[own, cols]
            send_part(k, j).wait_recv()
            produced = (mine + precv[k, :, cols].astype(jnp.float32)).astype(jnp.bfloat16)
            obuf[k, :, cols] = produced

            @pl.when(sec < last)
            def _():
                send_u(k, j).start()

            out_ref[0, k, :, cols] = produced

        @pl.when(sec < half - 1)
        def _():
            send_skip(k).start()

        return 0

    lax.fori_loop(0, patch_count, step, 0)

    def finish(k, _):
        for j in range(len(chunks)):
            relay_u(k, j).wait_send()
            send_part(k, j).wait_send()

            @pl.when(sec < last)
            def _():
                send_u(k, j).wait_send()

        @pl.when(sec < half - 1)
        def _():
            send_skip(k).wait_send()

        @pl.when(sec > half)
        def _():
            relay_skip(k).wait_send()

        return 0

    lax.fori_loop(0, patch_count, finish, 0)


def body(patches, stale_kv, qkv_weight, out_weight, skip_joined_weight, qk_gain, order, tile_index):
    patch_count, own_rows, width = patches.shape
    sections = lax.axis_size("sec")
    tile_rows, lanes = stale_kv.shape[2:]
    rows = own_rows * 2
    wide = -(-lanes // LANES) * LANES
    chunks = column_chunks(width, 2)
    half_width = HEAD_DIM // 2
    index = np.arange(wide) % HEAD_DIM
    inverse = 10000.0 ** (-(index % half_width).astype(np.float64) / half_width)
    sign = np.where(index < half_width, -1.0, 1.0)
    freq = jnp.asarray(np.stack([inverse, sign]).astype(np.float32))
    count = len(chunks)
    bf, f32 = jnp.bfloat16, jnp.float32
    vmem = pl.BlockSpec(memory_space=pltpu.VMEM)
    smem = pl.BlockSpec(memory_space=pltpu.SMEM)
    hbm = pl.BlockSpec(memory_space=pl.ANY)
    dma = pltpu.SemaphoreType.DMA
    dims = (sections, patch_count, own_rows, width, lanes, tile_rows, chunks)
    return pl.pallas_call(
        functools.partial(kernel, dims),
        out_shape=jax.ShapeDtypeStruct((1, patch_count, own_rows, width), bf),
        in_specs=[smem, smem, hbm, hbm, hbm, hbm, hbm, hbm, hbm],
        out_specs=vmem,
        scratch_shapes=[
            pltpu.VMEM(patches.shape, bf),
            pltpu.VMEM(qk_gain.shape, bf),
            pltpu.VMEM(freq.shape, f32),
            pltpu.VMEM((3, lanes, width), bf),
            pltpu.VMEM((lanes, width), bf),
            pltpu.VMEM((2 * width, width), bf),
            pltpu.VMEM((lanes, tile_rows), bf),
            pltpu.VMEM((lanes, tile_rows), bf),
            pltpu.VMEM((patch_count * rows, lanes), bf),
            pltpu.VMEM((patch_count * rows, lanes), bf),
            pltpu.VMEM((patch_count, rows, width), bf),
            pltpu.VMEM((patch_count, rows, width), bf),
            pltpu.VMEM((patch_count, rows, width), f32),
            pltpu.VMEM((rows, width), bf),
            pltpu.VMEM((rows, wide), f32),
            pltpu.VMEM((rows, wide), f32),
            pltpu.VMEM((rows, lanes), bf),
            pltpu.VMEM((rows, width), f32),
            pltpu.VMEM((patch_count, own_rows, width), bf),
            pltpu.VMEM((patch_count, own_rows, width), bf),
            pltpu.VMEM((patch_count, own_rows, width), bf),
            pltpu.VMEM((patch_count, rows, wide), f32),
            pltpu.VMEM((patch_count, rows, wide), f32),
            pltpu.VMEM((2, wide), f32),
            dma((3,)),
            dma((3,)),
            dma((2,)),
            dma,
            dma((2,)),
            dma((patch_count, count)),
            dma((patch_count, count)),
            dma((patch_count, count)),
            dma((patch_count, count)),
            dma((patch_count,)),
            dma((patch_count,)),
            dma((patch_count,)),
            dma((patch_count,)),
            dma((patch_count, count)),
            dma((patch_count, count)),
        ],
        compiler_params=pltpu.CompilerParams(
            collective_id=0, has_side_effects=True, vmem_limit_bytes=60 * 1024 * 1024
        ),
    )(order, tile_index, patches, qk_gain, freq, jnp.swapaxes(stale_kv, 2, 3), jnp.swapaxes(qkv_weight, 2, 3), out_weight, skip_joined_weight)


def solution(mesh):
    return jax.shard_map(
        body,
        mesh=mesh,
        in_specs=(
            P("grp", "head", None),
            P(("grp", "sec"), None, None, "head"),
            P("sec", None, None, "head"),
            P("sec", "head", None),
            P("sec", None, None),
            P("sec", None, "head"),
            P("grp"),
            P("grp"),
        ),
        out_specs=P("sec", "grp", "head", None),
        check_vma=False,
    )
```

```python
import functools
import math

import jax
import jax.numpy as jnp
import numpy as np
from jax import lax
from jax.experimental import pallas as pl
from jax.experimental.pallas import tpu as pltpu
from jax.sharding import PartitionSpec as P

HEAD_DIM = 88
EPSILON = 1e-06
LANES = 128
MESH = pl.DeviceIdType.MESH


def layer_norm(x):
    centred = x - jnp.mean(x, axis=-1, keepdims=True)
    variance = jnp.mean(centred * centred, axis=-1, keepdims=True)
    return centred * lax.rsqrt(variance + EPSILON)


def across(a, b):
    return lax.dot_general(a, b, (((1,), (1,)), ((), ())), preferred_element_type=jnp.float32)


def column_chunks(width, count):
    tiles = width // LANES
    step = -(-tiles // count)
    step += step % 2
    edges = list(range(0, tiles, step)) + [tiles]
    return [(a * LANES, (b - a) * LANES) for a, b in zip(edges[:-1], edges[1:])]


def kernel(
    dims,
    order_ref, tile_ref, patches_hbm, gain_hbm, freq_hbm, kv_hbm, wqkv_hbm, wout_hbm, wskip_hbm,
    out_ref,
    patches_ref, gain_ref, freq_ref, wqkv, wout, wskip, kbuf, vbuf, knew, vnew, ubuf, sbuf, pre, hsb, qs, ks, att, pbuf, psend, precv, obuf, cosb, sinb, gains,
    in_sem, w_sem, kv_sem, wo_sem, ws_sem,
    u_send, u_recv, r_send, r_recv, s_send, s_recv, t_send, t_recv, p_send, p_recv,
):
    sections, patch_count, own_rows, width, lanes, tile_rows, chunks = dims
    rows = own_rows * 2
    heads = lanes // HEAD_DIM
    wide = qs.shape[1]
    half = sections // 2
    last = sections - 1
    sec = lax.axis_index("sec")
    core = lax.axis_index("head")
    peer = 1 - core
    partner = last - sec
    own = pl.ds(pl.multiple_of(core * own_rows, own_rows), own_rows)
    other = pl.ds(pl.multiple_of(peer * own_rows, own_rows), own_rows)
    far_partner = (sec < half - 1) | (sec > half)

    w_copies = [pltpu.make_async_copy(wqkv_hbm.at[0, c], wqkv.at[c], w_sem.at[c]) for c in range(3)]
    k_copy = pltpu.make_async_copy(kv_hbm.at[0, 0], kbuf, kv_sem.at[0])
    v_copy = pltpu.make_async_copy(kv_hbm.at[0, 1], vbuf, kv_sem.at[1])
    o_copy = pltpu.make_async_copy(wout_hbm.at[0], wout, wo_sem)
    top_copy = pltpu.make_async_copy(wskip_hbm.at[0, pl.ds(0, width)], wskip.at[pl.ds(0, width)], ws_sem.at[0])
    low_copy = pltpu.make_async_copy(wskip_hbm.at[0, pl.ds(width, width)], wskip.at[pl.ds(width, width)], ws_sem.at[1])
    small = [
        pltpu.make_async_copy(patches_hbm, patches_ref, in_sem.at[0]),
        pltpu.make_async_copy(freq_hbm, freq_ref, in_sem.at[1]),
        pltpu.make_async_copy(gain_hbm, gain_ref, in_sem.at[2]),
    ]
    for copy in (*small, *w_copies, k_copy, v_copy, o_copy):
        copy.start()

    @pl.when(sec >= half)
    def _():
        low_copy.start()
        top_copy.start()

    barrier = pltpu.get_barrier_semaphore()
    pl.semaphore_signal(barrier, inc=1, device_id={"head": peer}, device_id_type=MESH)

    @pl.when(sec < last)
    def _():
        pl.semaphore_signal(barrier, inc=1, device_id={"sec": sec + 1}, device_id_type=MESH)

    @pl.when(sec > 0)
    def _():
        pl.semaphore_signal(barrier, inc=1, device_id={"sec": sec - 1}, device_id_type=MESH)

    @pl.when(far_partner)
    def _():
        pl.semaphore_signal(barrier, inc=1, device_id={"sec": partner}, device_id_type=MESH)

    greeted = (
        1
        + jnp.where(sec < last, 1, 0)
        + jnp.where(sec > 0, 1, 0)
        + jnp.where(far_partner, 1, 0)
    )
    pl.semaphore_wait(barrier, greeted)

    def relay_u(k, j):
        start, size = chunks[j]
        piece = ubuf.at[k, own, pl.ds(start, size)]
        return pltpu.make_async_remote_copy(
            piece, piece, r_send.at[k, j], r_recv.at[k, j], device_id={"head": peer}, device_id_type=MESH
        )

    def send_u(k, j):
        start, size = chunks[j]
        return pltpu.make_async_remote_copy(
            obuf.at[k, :, pl.ds(start, size)],
            ubuf.at[k, own, pl.ds(start, size)],
            u_send.at[k, j],
            u_recv.at[k, j],
            device_id={"sec": jnp.minimum(sec + 1, last)},
            device_id_type=MESH,
        )

    def send_skip(k):
        return pltpu.make_async_remote_copy(
            obuf.at[k], sbuf.at[k, own], s_send.at[k], s_recv.at[k], device_id={"sec": partner}, device_id_type=MESH
        )

    def relay_skip(k):
        piece = sbuf.at[k, own]
        return pltpu.make_async_remote_copy(
            piece, piece, t_send.at[k], t_recv.at[k], device_id={"head": peer}, device_id_type=MESH
        )

    def send_part(k, j):
        start, size = chunks[j]
        return pltpu.make_async_remote_copy(
            psend.at[k, :, pl.ds(start, size)],
            precv.at[k, :, pl.ds(start, size)],
            p_send.at[k, j],
            p_recv.at[k, j],
            device_id={"head": peer},
            device_id_type=MESH,
        )

    for copy in small:
        copy.wait()

    @pl.when(sec == 0)
    def _():
        for k in range(patch_count):
            ubuf[k, own, :] = patches_ref[k]

    tiles = [(t, min(LANES, lanes - t)) for t in range(0, lanes, LANES)]
    lane = [lax.broadcasted_iota(jnp.int32, (1, LANES), 1) + t for t, _ in tiles]

    def spans(h):
        return [t for t in range(len(tiles)) if t * LANES < (h + 1) * HEAD_DIM and (t + 1) * LANES > h * HEAD_DIM]

    def mask(h, t):
        return (lane[t] >= h * HEAD_DIM) & (lane[t] < (h + 1) * HEAD_DIM)

    def tables(k, _):
        start = tile_ref[0] * tile_rows + order_ref[k] * rows
        position = (lax.broadcasted_iota(jnp.int32, (rows, LANES), 0) + start).astype(jnp.float32)
        for t in range(len(tiles)):
            cols = pl.ds(t * LANES, LANES)
            angle = position * freq_ref[0:1, cols]
            cosb[k, :, cols] = jnp.cos(angle)
            sinb[k, :, cols] = jnp.sin(angle) * freq_ref[1:2, cols]
        return 0

    lax.fori_loop(0, patch_count, tables, 0)
    qs[...] = jnp.zeros_like(qs)
    ks[...] = jnp.zeros_like(ks)
    gains[...] = jnp.zeros_like(gains)
    gains[:, pl.ds(0, lanes)] = gain_ref[0].astype(jnp.float32)
    knew[...] = jnp.zeros_like(knew)
    vnew[...] = jnp.zeros_like(vnew)

    @pl.when(sec >= half)
    def _():
        low_copy.wait()

    @pl.when(sec == half)
    def _():
        pre[...] = jnp.zeros_like(pre)

    @pl.when(sec > half)
    def _():
        def ahead(k, _):
            relay = relay_skip(k)
            send_skip(k).wait_recv()
            relay.start()
            relay.wait_recv()
            pre[k] = jnp.dot(sbuf[k], wskip[pl.ds(width, width), :], preferred_element_type=jnp.float32)
            return 0

        lax.fori_loop(0, patch_count, ahead, 0)

    @pl.when(sec >= half)
    def _():
        top_copy.wait()

    def head_sums(parts):
        sums = [None] * heads
        for h in range(heads):
            total = None
            for t in spans(h):
                term = jnp.where(mask(h, t), parts[t], 0.0)
                total = term if total is None else total + term
            sums[h] = jnp.sum(total, axis=1, keepdims=True) * (1.0 / HEAD_DIM)
        result = []
        for t in range(len(tiles)):
            value = jnp.zeros((rows, LANES), jnp.float32)
            for h in range(heads):
                if t in spans(h):
                    value = jnp.where(mask(h, t), sums[h], value)
            result.append(value)
        return result

    def head_norm(buf, which, k):
        parts = [buf[:, pl.ds(t * LANES, LANES)] for t in range(len(tiles))]
        means = head_sums(parts)
        parts = [a - m for a, m in zip(parts, means)]
        variances = head_sums([a * a for a in parts])
        for t in range(len(tiles)):
            cols = pl.ds(t * LANES, LANES)
            buf[:, cols] = parts[t] * lax.rsqrt(variances[t] + EPSILON) * gains[which : which + 1, cols]
        value = buf[...]
        ahead = pltpu.roll(value, wide - HEAD_DIM // 2, 1)
        behind = pltpu.roll(value, HEAD_DIM // 2, 1)
        turned = jnp.where(freq_ref[1:2, :] < 0.0, ahead, behind)
        return value * cosb[k] + turned * sinb[k]

    def step(k, _):
        for j in range(len(chunks)):
            @pl.when(sec > 0)
            def _():
                send_u(k, j).wait_recv()

            relay_u(k, j).start()
        for j, (begin, size) in enumerate(chunks):
            relay_u(k, j).wait_recv()
            cols = pl.ds(begin, size)

            @pl.when(sec == half)
            def _():
                pre[k] += jnp.dot(ubuf[k, :, cols], wskip[pl.ds(width + begin, size), :], preferred_element_type=jnp.float32)

            @pl.when(sec >= half)
            def _():
                pre[k] += jnp.dot(ubuf[k, :, cols], wskip[cols, :], preferred_element_type=jnp.float32)

        @pl.when(sec < half)
        def _():
            hsb[...] = ubuf[k]

        @pl.when(sec >= half)
        def _():
            hsb[...] = layer_norm(pre[k]).astype(jnp.bfloat16)

        normed = layer_norm(hsb[...].astype(jnp.float32)).astype(jnp.bfloat16)

        @pl.when(k == 0)
        def _():
            for copy in (*w_copies, k_copy, v_copy, o_copy):
                copy.wait()

        qs[:, pl.ds(0, lanes)] = across(normed, wqkv[0])
        ks[:, pl.ds(0, lanes)] = across(normed, wqkv[1])
        fresh = pl.ds(pl.multiple_of(k * rows, rows), rows)
        vnew[fresh, :] = across(normed, wqkv[2]).astype(jnp.bfloat16)
        q_rot = head_norm(qs, 0, k)
        k_rot = head_norm(ks, 1, k)
        knew[fresh, :] = k_rot[:, :lanes].astype(jnp.bfloat16)

        slot = lax.broadcasted_iota(jnp.int32, (1, tile_rows), 1) // rows
        gone = slot < 0
        for i in range(patch_count):
            gone = gone | ((slot == order_ref[i]) & (i <= k))
        keep = jnp.where(gone, -1e30, 0.0)
        source = lax.broadcasted_iota(jnp.int32, (1, patch_count * rows), 1) // rows
        keep_new = jnp.where(source > k, -1e30, 0.0)
        scale = math.log2(math.e) / math.sqrt(HEAD_DIM)
        q_rot = q_rot * scale
        mixed_tiles = [None] * len(tiles)
        for h in range(heads):
            found = spans(h)
            low = found[0] * LANES
            span = min(lanes, (found[-1] + 1) * LANES) - low
            query = jnp.concatenate(
                [jnp.where(mask(h, t), q_rot[:, t * LANES : (t + 1) * LANES], 0.0) for t in found], axis=1
            )[:, :span].astype(jnp.bfloat16)
            window = pl.ds(low, span)
            scores = jnp.dot(query, kbuf[window, :], preferred_element_type=jnp.float32)
            scores_new = across(query, knew[:, window])
            expd = jnp.exp2(scores + keep)
            expd_new = jnp.exp2(scores_new + keep_new)
            total = jnp.sum(expd, axis=1, keepdims=True) + jnp.sum(expd_new, axis=1, keepdims=True)
            mixed = across(expd.astype(jnp.bfloat16), vbuf[window, :]) + jnp.dot(
                expd_new.astype(jnp.bfloat16), vnew[:, window], preferred_element_type=jnp.float32
            )
            mixed = mixed * (1.0 / total)
            for t in found:
                size = tiles[t][1]
                value = mixed[:, t * LANES - low : t * LANES - low + size]
                before = mixed_tiles[t]
                mixed_tiles[t] = value if before is None else jnp.where(mask(h, t)[:, :size], value, before)
        for t, (begin, size) in enumerate(tiles):
            att[:, pl.ds(begin, size)] = mixed_tiles[t].astype(jnp.bfloat16)

        for j, (begin, size) in enumerate(chunks):
            cols = pl.ds(begin, size)
            pbuf[:, cols] = jnp.dot(att[...], wout[:, cols], preferred_element_type=jnp.float32)
            psend[k, :, cols] = pbuf[other, cols].astype(jnp.bfloat16)
            send_part(k, j).start()
        for j, (begin, size) in enumerate(chunks):
            cols = pl.ds(begin, size)
            mine = hsb[own, cols].astype(jnp.float32) + pbuf[own, cols]
            send_part(k, j).wait_recv()
            produced = (mine + precv[k, :, cols].astype(jnp.float32)).astype(jnp.bfloat16)
            obuf[k, :, cols] = produced

            @pl.when(sec < last)
            def _():
                send_u(k, j).start()

            out_ref[0, k, :, cols] = produced

        @pl.when(sec < half - 1)
        def _():
            send_skip(k).start()

        return 0

    lax.fori_loop(0, patch_count, step, 0)

    def finish(k, _):
        for j in range(len(chunks)):
            relay_u(k, j).wait_send()
            send_part(k, j).wait_send()

            @pl.when(sec < last)
            def _():
                send_u(k, j).wait_send()

        @pl.when(sec < half - 1)
        def _():
            send_skip(k).wait_send()

        @pl.when(sec > half)
        def _():
            relay_skip(k).wait_send()

        return 0

    lax.fori_loop(0, patch_count, finish, 0)


def body(patches, stale_kv, qkv_weight, out_weight, skip_joined_weight, qk_gain, order, tile_index):
    patch_count, own_rows, width = patches.shape
    sections = lax.axis_size("sec")
    tile_rows, lanes = stale_kv.shape[2:]
    rows = own_rows * 2
    wide = -(-lanes // LANES) * LANES
    chunks = column_chunks(width, 2)
    half_width = HEAD_DIM // 2
    index = np.arange(wide) % HEAD_DIM
    inverse = 10000.0 ** (-(index % half_width).astype(np.float64) / half_width)
    sign = np.where(index < half_width, -1.0, 1.0)
    freq = jnp.asarray(np.stack([inverse, sign]).astype(np.float32))
    count = len(chunks)
    bf, f32 = jnp.bfloat16, jnp.float32
    vmem = pl.BlockSpec(memory_space=pltpu.VMEM)
    smem = pl.BlockSpec(memory_space=pltpu.SMEM)
    hbm = pl.BlockSpec(memory_space=pl.ANY)
    dma = pltpu.SemaphoreType.DMA
    dims = (sections, patch_count, own_rows, width, lanes, tile_rows, chunks)
    return pl.pallas_call(
        functools.partial(kernel, dims),
        out_shape=jax.ShapeDtypeStruct((1, patch_count, own_rows, width), bf),
        in_specs=[smem, smem, hbm, hbm, hbm, hbm, hbm, hbm, hbm],
        out_specs=vmem,
        scratch_shapes=[
            pltpu.VMEM(patches.shape, bf),
            pltpu.VMEM(qk_gain.shape, bf),
            pltpu.VMEM(freq.shape, f32),
            pltpu.VMEM((3, lanes, width), bf),
            pltpu.VMEM((lanes, width), bf),
            pltpu.VMEM((2 * width, width), bf),
            pltpu.VMEM((lanes, tile_rows), bf),
            pltpu.VMEM((lanes, tile_rows), bf),
            pltpu.VMEM((patch_count * rows, lanes), bf),
            pltpu.VMEM((patch_count * rows, lanes), bf),
            pltpu.VMEM((patch_count, rows, width), bf),
            pltpu.VMEM((patch_count, rows, width), bf),
            pltpu.VMEM((patch_count, rows, width), f32),
            pltpu.VMEM((rows, width), bf),
            pltpu.VMEM((rows, wide), f32),
            pltpu.VMEM((rows, wide), f32),
            pltpu.VMEM((rows, lanes), bf),
            pltpu.VMEM((rows, width), f32),
            pltpu.VMEM((patch_count, own_rows, width), bf),
            pltpu.VMEM((patch_count, own_rows, width), bf),
            pltpu.VMEM((patch_count, own_rows, width), bf),
            pltpu.VMEM((patch_count, rows, wide), f32),
            pltpu.VMEM((patch_count, rows, wide), f32),
            pltpu.VMEM((2, wide), f32),
            dma((3,)),
            dma((3,)),
            dma((2,)),
            dma,
            dma((2,)),
            dma((patch_count, count)),
            dma((patch_count, count)),
            dma((patch_count, count)),
            dma((patch_count, count)),
            dma((patch_count,)),
            dma((patch_count,)),
            dma((patch_count,)),
            dma((patch_count,)),
            dma((patch_count, count)),
            dma((patch_count, count)),
        ],
        compiler_params=pltpu.CompilerParams(
            collective_id=0, has_side_effects=True, vmem_limit_bytes=60 * 1024 * 1024
        ),
    )(order, tile_index, patches, qk_gain, freq, jnp.swapaxes(stale_kv, 2, 3), jnp.swapaxes(qkv_weight, 2, 3), out_weight, skip_joined_weight)


def solution(mesh):
    return jax.shard_map(
        body,
        mesh=mesh,
        in_specs=(
            P("grp", "head", None),
            P(("grp", "sec"), None, None, "head"),
            P("sec", None, None, "head"),
            P("sec", "head", None),
            P("sec", None, None),
            P("sec", None, "head"),
            P("grp"),
            P("grp"),
        ),
        out_specs=P("sec", "grp", "head", None),
        check_vma=False,
    )
```
